32 devices in a mesh: br: 16 (over z, y, x), bus: 2 (over core).
Axes of the slice: x: 2, y: 2, z: 4, core: 2. Of those that a mesh axis runs over, the one named last changes fastest.
Arguments:
- net_load: bfloat16 [128, 60416], P('br', 'bus'), may hold values from -6 to 6
- release: float32 [128, 1024], P('br'), may hold values from 0 to 2
- plant_bus: int32 [1024], replicated, may hold values from 0 to 60415
- efficiency: float32 [1024], replicated, may hold values from 0.5 to 2
- ptdf: bfloat16 [2048, 60416], P('br', 'bus'), may hold values from -0.0234375 to 0.0234375
- branch_class: int32 [2048], P('br'), may hold values from 0 to 15
- class_limit: float32 [16], replicated, may hold values from 0.4 to 3
- class_price: float32 [16], replicated, may hold values from 0.5 to 5
Outputs:
- grad_bus: float32 [128, 60416], P('br', 'bus')
- grad_release: float32 [128, 1024], P('br')
The draws below stay inside these ranges and needn't reach their ends.
All inputs are finite; a program needn't handle non-finite values.
Results may differ from the reference program's by a relative error of at most 0.0031.
Values may be sent and summed in bfloat16 or wider, within the bound.
No kernel may reach another device: no remote copies, remote signals or barrier semaphores. Data moves between devices by JAX's collectives and lax.ppermute only.
A program may use at most 64 MiB of HBM per device.

```python
import math
import jax
import jax.numpy as jnp
from jax import lax

BUSES = 60416
BRANCHES = 2048
SCEN = 128
PLANTS = 1024
CLASSES = 16


def with_ends(array, stream_key, least, high):
    shape = array.shape
    index_at = [jax.random.randint(jax.random.fold_in(stream_key, axis), (), 0, shape[axis]) for axis in range(len(shape))]
    array = array.at[tuple(index_at)].set(least)
    longest = shape.index(max(shape))
    index_at[longest] = (index_at[longest] + 1) % shape[longest]
    return array.at[tuple(index_at)].set(high)


def shard_levels(rng, shape, split, smallest, high):
    def one(position, parts):
        draws = jax.random.uniform(jax.random.fold_in(jax.random.fold_in(rng, 6), position), (parts,), jnp.float32, smallest / len(split), high / len(split))
        return jnp.repeat(jnp.exp(draws), shape[position] // parts).reshape((-1,) + (1,) * (len(shape) - position - 1))

    level = one(*split[0])
    for cut in split[1:]:
        level = level * one(*cut)
    return level


def gaussian(stream_key, shape, width, bound, cuts=(), dtype=jnp.bfloat16):
    factor_of = shard_levels(stream_key, shape, cuts, -0.22, 0.18) if cuts else 1.0
    array = jax.random.normal(stream_key, shape, jnp.float32) * width * factor_of
    return jnp.minimum(jnp.maximum(array, -bound), bound).astype(dtype)


def setup_inputs(seed: int = 0) -> dict:
    seeds = jax.random.split(jax.random.key(seed), 9)
    net_load = gaussian(seeds[0], (SCEN, BUSES), 1.0, 6.0, ((0, 16), (1, 2)))
    release = jnp.clip(2.0 * jax.random.uniform(seeds[1], (SCEN, PLANTS), jnp.float32) ** shard_levels(seeds[1], (SCEN, PLANTS), ((0, 16),), -0.2, 0.2), 0.0, 2.0)
    plant_bus = with_ends(jax.random.randint(seeds[2], (PLANTS,), 0, BUSES), jax.random.fold_in(seeds[2], 1), 0, BUSES - 1).astype(jnp.int32)
    efficiency = jnp.clip(jnp.exp(jax.random.uniform(seeds[3], (PLANTS,), jnp.float32, math.log(0.5), math.log(2.0))), 0.5, 2.0)
    ptdf = gaussian(seeds[4], (BRANCHES, BUSES), BUSES ** -0.5, 0.0234375, ((0, 16), (1, 2)))
    branch_class = with_ends(jax.random.randint(seeds[5], (BRANCHES,), 0, CLASSES), jax.random.fold_in(seeds[5], 1), 0, CLASSES - 1).astype(jnp.int32)
    class_limit = jnp.clip(jnp.exp(jax.random.uniform(seeds[6], (CLASSES,), jnp.float32, math.log(0.4), math.log(3.0))), 0.4, 3.0)
    class_price = jnp.clip(jnp.exp(jax.random.uniform(seeds[7], (CLASSES,), jnp.float32, math.log(0.5), math.log(5.0))), 0.5, 5.0)
    return dict(net_load=net_load, release=release, plant_bus=plant_bus, efficiency=efficiency, ptdf=ptdf, branch_class=branch_class, class_limit=class_limit, class_price=class_price)


SMOOTH = 0.25


def reference(net_load, release, plant_bus, efficiency, ptdf, branch_class, class_limit, class_price):
    inject = net_load.astype(jnp.float32).at[:, plant_bus].add(release * efficiency[None, :]).astype(jnp.bfloat16)
    flows = lax.dot_general(inject, ptdf, (((1,), (1,)), ((), ())), preferred_element_type=jnp.float32)
    limit = class_limit[branch_class][None, :]
    price = class_price[branch_class][None, :]
    grad_flow = (price * (jax.nn.sigmoid((flows - limit) / SMOOTH) - jax.nn.sigmoid((-flows - limit) / SMOOTH))).astype(jnp.bfloat16)
    grad_bus = jnp.dot(grad_flow, ptdf, preferred_element_type=jnp.float32)
    grad_release = grad_bus[:, plant_bus] * efficiency[None, :]
    return grad_bus, grad_release
```

```python
import functools

import jax
import jax.numpy as jnp
from jax import lax
from jax.experimental import pallas as pl
from jax.experimental.pallas import tpu as pltpu
from jax.sharding import PartitionSpec as P

SMOOTH = 0.25
Z, Y, X = 0, 1, 2


def chip_box(count):
    bits = (count // 2).bit_length() - 1
    nx = 1 << (bits // 2)
    return count // (2 * nx), 2, nx


GATHER = [
    [(Z, -1, (-1, 0, 0)), (X, 1, (0, 0, 1)), (Y, 1, (0, 1, 0))],
    [(Z, -1, (2, 0, 0)), (X, 1, (-1, 0, 1)), (Y, 1, (0, 1, 1))],
    [(Z, 1, (1, 1, 0)), (X, 1, (2, 0, 1)), (Y, 1, (-1, 1, 1))],
    [(Z, 1, (1, 0, 0)), (X, 1, (1, 1, 1)), (Y, 1, (2, 1, 1))],
    [(Z, 1, (2, 1, 0)), (X, 1, (1, 0, 1)), (Y, 1, (-1, 1, 0))],
]
REDUCE = [
    [(Z, 1, (1, 0, 0)), (X, 1, (0, 0, 1)), (Y, 1, (0, 1, 0))],
    [(Z, 1, (2, 0, 0)), (X, 1, (1, 0, 1)), (Y, 1, (1, 1, 0))],
    [(Z, -1, (-1, 1, 0)), (X, 1, (2, 0, 1)), (Y, 1, (2, 1, 0))],
    [(Z, -1, (-1, 0, 0)), (X, 1, (1, 1, 1)), (Y, 1, (2, 1, 1))],
    [(Z, -1, (-1, 0, 1)), (X, 1, (-1, 1, 1)), (Y, 1, (0, 1, 1))],
]
BATCH_ENDS = (2, 3, 4)


def greedy(box):
    labels = [(z, y, x) for z in range(box[0]) for y in range(box[1]) for x in range(box[2])]
    have, rounds = {(0, 0, 0)}, []
    while len(have) < len(labels):
        taken, now = set(), []
        for axis in (Z, X, Y):
            shifts = (1, -1) if box[axis] > 2 else (1,)
            options = [
                (shift, label)
                for label in labels
                if label not in have and label not in taken
                for shift in shifts
                if step_back(label, axis, shift, box) in have
            ]
            if options:
                shift, label = options[0]
                now.append((axis, shift, label))
                taken.add(label)
        have |= taken
        rounds.append(now)
    return rounds


def step_back(label, axis, shift, box):
    moved = list(label)
    moved[axis] = (moved[axis] - shift) % box[axis]
    return tuple(moved)


def plan(box):
    if box == (4, 2, 2):
        wrap = lambda rounds: [
            [(a, s, tuple(c % n for c, n in zip(label, box))) for a, s, label in now] for now in rounds
        ]
        return wrap(GATHER), wrap(REDUCE), BATCH_ENDS
    rounds = greedy(box)
    return rounds, rounds, (len(rounds) - 1,)


def moves(axis, shift, box):
    pairs = []
    for z in range(box[0]):
        for y in range(box[1]):
            for x in range(box[2]):
                to = step_back((z, y, x), axis, -shift, box)
                pairs.append(((z * box[1] + y) * box[2] + x, (to[0] * box[1] + to[1]) * box[2] + to[2]))
    return pairs


def after(value, earlier):
    if earlier is None:
        return value
    return lax.optimization_barrier((value, earlier))[0]


def tile_of(width):
    groups = width // 128
    return 128 * max(n for n in range(1, 65) if groups % n == 0)


def inject_kernel(net_ref, weight_ref, column_ref, out_ref):
    rows, width = net_ref.shape
    groups = width // 128
    column = column_ref[...]
    place = jnp.where(column >= 0, column // 128, -1) - pl.program_id(0) * groups
    weight = weight_ref[...]
    high = weight.astype(jnp.bfloat16).astype(jnp.float32)
    low = weight - high
    lane = lax.broadcasted_iota(jnp.int32, (128, column.shape[1]), 0)
    lanes = jnp.where(lane == column % 128, 1.0, 0.0).astype(jnp.bfloat16)

    def spread(values):
        picked = [jnp.where(place == group, values, 0.0) for group in range(groups)]
        return lax.dot_general(
            jnp.concatenate(picked, axis=0).astype(jnp.bfloat16),
            lanes,
            (((1,), (1,)), ((), ())),
            preferred_element_type=jnp.float32,
        )

    added = spread(high) + spread(low)
    for group in range(groups):
        at = slice(group * 128, (group + 1) * 128)
        total = net_ref[:, at].astype(jnp.float32) + added[group * rows : (group + 1) * rows]
        out_ref[:, at] = total.astype(jnp.bfloat16)


def inject_of(net_load, weight, column):
    rows, width = net_load.shape
    short = -rows % 8
    if short:
        net_load = jnp.pad(net_load, ((0, short), (0, 0)))
        weight = jnp.pad(weight, ((0, short), (0, 0)))
    tile = tile_of(width)
    plants = weight.shape[1]
    out = pl.pallas_call(
        inject_kernel,
        grid=(width // tile,),
        in_specs=[
            pl.BlockSpec((rows + short, tile), lambda i: (0, i)),
            pl.BlockSpec((rows + short, plants), lambda i: (0, 0)),
            pl.BlockSpec((1, plants), lambda i: (0, 0)),
        ],
        out_specs=pl.BlockSpec((rows + short, tile), lambda i: (0, i)),
        out_shape=jax.ShapeDtypeStruct(net_load.shape, jnp.bfloat16),
        compiler_params=pltpu.CompilerParams(vmem_limit_bytes=32 << 20),
        name="inject",
    )(net_load, weight, column)
    return out[:rows] if short else out


def flows_kernel(count, *refs):
    blocks, ptdf_ref, out_ref = refs[:count], refs[count], refs[count + 1]

    @pl.when(pl.program_id(0) == 0)
    def _():
        out_ref[...] = jnp.zeros_like(out_ref)

    rows = jnp.concatenate([block[...].astype(jnp.float32) for block in blocks], axis=0)
    out_ref[...] += lax.dot_general(
        rows.astype(jnp.bfloat16), ptdf_ref[...], (((1,), (1,)), ((), ())), preferred_element_type=jnp.float32
    )


def flows_of(blocks, ptdf):
    rows, width = blocks[0].shape
    branches = ptdf.shape[0]
    if rows % 8:
        blocks = [jnp.pad(jnp.concatenate(blocks, axis=0), ((0, -rows * len(blocks) % 8), (0, 0)))]
    count = len(blocks)
    tile = tile_of(width)
    total = sum(block.shape[0] for block in blocks)
    return pl.pallas_call(
        functools.partial(flows_kernel, count),
        grid=(width // tile,),
        in_specs=[pl.BlockSpec((block.shape[0], tile), lambda i: (0, i)) for block in blocks]
        + [pl.BlockSpec((branches, tile), lambda i: (0, i))],
        out_specs=pl.BlockSpec((total, branches), lambda i: (0, 0)),
        out_shape=jax.ShapeDtypeStruct((total, branches), jnp.float32),
        compiler_params=pltpu.CompilerParams(vmem_limit_bytes=32 << 20),
        cost_estimate=pl.CostEstimate(
            flops=2 * total * branches * width, bytes_accessed=2 * (total + branches) * width, transcendentals=0
        ),
        name="flows",
    )(*blocks, ptdf)


def make_shards(box, buses):
    gather, reduce, ends = plan(box)
    own = (0, 0, 0)

    def shards(net_load, release, plant_bus, efficiency, ptdf, branch_class, class_limit, class_price):
        rows_local, bus_local = net_load.shape
        offset = lax.axis_index("bus") * bus_local
        columns = plant_bus - offset
        inside = ((columns >= 0) & (columns < bus_local)).astype(jnp.float32)
        clipped = jnp.clip(columns, 0, bus_local - 1)
        weighted = efficiency * inside
        inject = inject_of(net_load, release * weighted[None, :], jnp.where(inside > 0, columns, -1)[None, :])
        onehot = (branch_class[:, None] == jnp.arange(class_limit.shape[0])[None, :]).astype(jnp.float32)
        limit = jnp.sum(onehot * class_limit[None, :], axis=1)[None, :]
        price = jnp.sum(onehot * class_price[None, :], axis=1)[None, :]

        def partial_grads(blocks):
            flows = flows_of(blocks, ptdf)
            if buses == 2:
                flows = flows + lax.ppermute(flows, "bus", [(0, 1), (1, 0)])
            else:
                flows = lax.psum(flows, "bus")
            upper = jax.nn.sigmoid((flows - limit) / SMOOTH)
            lower = jax.nn.sigmoid((-flows - limit) / SMOOTH)
            grad_flow = (price * (upper - lower)).astype(jnp.bfloat16)
            part = jnp.dot(grad_flow, ptdf, preferred_element_type=jnp.float32)
            return [part[i * rows_local : (i + 1) * rows_local] for i in range(len(blocks))]

        have, parts, fresh, last = {own: inject}, {}, [own], {}
        for index, now in enumerate(gather):
            for axis, shift, label in now:
                block = after(have[step_back(label, axis, shift, box)], last.get(axis))
                have[label] = last[axis] = lax.ppermute(block, "br", moves(axis, shift, box))
                fresh.append(label)
            if index in ends:
                for label, part in zip(fresh, partial_grads([have[label] for label in fresh])):
                    parts[label] = part
                fresh = []

        for now in reversed(reduce):
            for axis, shift, label in reversed(now):
                block = after(parts[label].astype(jnp.bfloat16), last.get(axis))
                last[axis] = lax.ppermute(block, "br", moves(axis, -shift, box))
                to = step_back(label, axis, shift, box)
                parts[to] = parts[to] + last[axis].astype(jnp.float32)
        grad_bus = parts[own]
        picked = grad_bus[:, clipped] * weighted[None, :]
        grad_release = lax.psum(picked, "bus")
        return (grad_bus, grad_release)

    return shards


def solution(mesh):
    placed = (P("br", "bus"), P("br", None), P(), P(), P("br", "bus"), P("br"), P(), P())
    return jax.shard_map(
        make_shards(chip_box(mesh.shape["br"]), mesh.shape["bus"]),
        mesh=mesh,
        in_specs=placed,
        out_specs=(P("br", "bus"), P("br", None)),
        check_vma=False,
    )
```

```python
import functools

import jax
import jax.numpy as jnp
from jax import lax
from jax.experimental import pallas as pl
from jax.experimental.pallas import tpu as pltpu
from jax.sharding import PartitionSpec as P

SMOOTH = 0.25
Z, Y, X = 0, 1, 2


def chip_box(count):
    bits = (count // 2).bit_length() - 1
    nx = 1 << (bits // 2)
    return count // (2 * nx), 2, nx


GATHER = [
    [(Z, -1, (-1, 0, 0)), (X, 1, (0, 0, 1)), (Y, 1, (0, 1, 0))],
    [(Z, -1, (2, 0, 0)), (X, 1, (-1, 0, 1)), (Y, 1, (0, 1, 1))],
    [(Z, 1, (1, 1, 0)), (X, 1, (2, 0, 1)), (Y, 1, (-1, 1, 1))],
    [(Z, 1, (1, 0, 0)), (X, 1, (1, 1, 1)), (Y, 1, (2, 1, 1))],
    [(Z, 1, (2, 1, 0)), (X, 1, (1, 0, 1)), (Y, 1, (-1, 1, 0))],
]
REDUCE = [
    [(Z, 1, (1, 0, 0)), (X, 1, (0, 0, 1)), (Y, 1, (0, 1, 0))],
    [(Z, 1, (2, 0, 0)), (X, 1, (1, 0, 1)), (Y, 1, (1, 1, 0))],
    [(Z, -1, (-1, 1, 0)), (X, 1, (2, 0, 1)), (Y, 1, (2, 1, 0))],
    [(Z, -1, (-1, 0, 0)), (X, 1, (1, 1, 1)), (Y, 1, (2, 1, 1))],
    [(Z, -1, (-1, 0, 1)), (X, 1, (-1, 1, 1)), (Y, 1, (0, 1, 1))],
]
BATCH_ENDS = (2, 3, 4)


def greedy(box):
    labels = [(z, y, x) for z in range(box[0]) for y in range(box[1]) for x in range(box[2])]
    have, rounds = {(0, 0, 0)}, []
    while len(have) < len(labels):
        taken, now = set(), []
        for axis in (Z, X, Y):
            shifts = (1, -1) if box[axis] > 2 else (1,)
            options = [
                (shift, label)
                for label in labels
                if label not in have and label not in taken
                for shift in shifts
                if step_back(label, axis, shift, box) in have
            ]
            if options:
                shift, label = options[0]
                now.append((axis, shift, label))
                taken.add(label)
        have |= taken
        rounds.append(now)
    return rounds


def step_back(label, axis, shift, box):
    moved = list(label)
    moved[axis] = (moved[axis] - shift) % box[axis]
    return tuple(moved)


def plan(box):
    if box == (4, 2, 2):
        wrap = lambda rounds: [
            [(a, s, tuple(c % n for c, n in zip(label, box))) for a, s, label in now] for now in rounds
        ]
        return wrap(GATHER), wrap(REDUCE), BATCH_ENDS
    rounds = greedy(box)
    return rounds, rounds, (len(rounds) - 1,)


def moves(axis, shift, box):
    pairs = []
    for z in range(box[0]):
        for y in range(box[1]):
            for x in range(box[2]):
                to = step_back((z, y, x), axis, -shift, box)
                pairs.append(((z * box[1] + y) * box[2] + x, (to[0] * box[1] + to[1]) * box[2] + to[2]))
    return pairs


def after(value, earlier):
    if earlier is None:
        return value
    return lax.optimization_barrier((value, earlier))[0]


def tile_of(width):
    groups = width // 128
    return 128 * max(n for n in range(1, 65) if groups % n == 0)


def scatter_lanes(column):
    lane = lax.broadcasted_iota(jnp.int32, (128, column.shape[1]), 0)
    return jnp.where(lane == column % 128, 1.0, 0.0).astype(jnp.bfloat16)


def split_high(value):
    high = value.astype(jnp.bfloat16)
    return high, (value - high.astype(jnp.float32)).astype(jnp.bfloat16)


def inject_kernel(bus_ref, net_ref, release_ref, efficiency_ref, plant_ref, out_ref):
    rows, width = net_ref.shape
    groups = width // 128
    column = plant_ref[...]
    place = column // 128 - (bus_ref[0] * pl.num_programs(0) + pl.program_id(0)) * groups
    weight = release_ref[...] * efficiency_ref[...]
    lanes = scatter_lanes(column)

    def spread(values):
        picked = [jnp.where(place == group, values, 0.0) for group in range(groups)]
        return lax.dot_general(
            jnp.concatenate(picked, axis=0).astype(jnp.bfloat16),
            lanes,
            (((1,), (1,)), ((), ())),
            preferred_element_type=jnp.float32,
        )

    high, low = split_high(weight)
    added = spread(high.astype(jnp.float32)) + spread(low.astype(jnp.float32))
    for group in range(groups):
        at = slice(group * 128, (group + 1) * 128)
        total = net_ref[:, at].astype(jnp.float32) + added[group * rows : (group + 1) * rows]
        out_ref[:, at] = total.astype(jnp.bfloat16)


FREE = pl.CostEstimate(flops=0, bytes_accessed=0, transcendentals=0)
LARGE = pltpu.CompilerParams(vmem_limit_bytes=20 << 20)


def inject_of(bus, net_load, release, efficiency, plant_bus):
    rows, width = net_load.shape
    short = -rows % 8
    if short:
        net_load = jnp.pad(net_load, ((0, short), (0, 0)))
        release = jnp.pad(release, ((0, short), (0, 0)))
    tile = tile_of(width)
    plants = release.shape[1]
    whole = pl.BlockSpec((1, plants), lambda i: (0, 0))
    out = pl.pallas_call(
        inject_kernel,
        grid=(width // tile,),
        in_specs=[
            pl.BlockSpec(memory_space=pltpu.SMEM),
            pl.BlockSpec((rows + short, tile), lambda i: (0, i)),
            pl.BlockSpec((rows + short, plants), lambda i: (0, 0)),
            whole,
            whole,
        ],
        out_specs=pl.BlockSpec((rows + short, tile), lambda i: (0, i)),
        out_shape=jax.ShapeDtypeStruct(net_load.shape, jnp.bfloat16),
        compiler_params=LARGE,
        cost_estimate=FREE,
        name="inject",
    )(bus, net_load, release, efficiency[None, :], plant_bus[None, :])
    return out[:rows] if short else out


def flows_kernel(count, *refs):
    blocks, ptdf_ref, out_ref = refs[:count], refs[count], refs[count + 1]

    @pl.when(pl.program_id(0) == 0)
    def _():
        out_ref[...] = jnp.zeros_like(out_ref)

    rows = jnp.concatenate([block[...].astype(jnp.float32) for block in blocks], axis=0)
    out_ref[...] += lax.dot_general(
        rows.astype(jnp.bfloat16), ptdf_ref[...], (((1,), (1,)), ((), ())), preferred_element_type=jnp.float32
    )


def flows_of(blocks, ptdf):
    rows, width = blocks[0].shape
    branches = ptdf.shape[0]
    if rows % 8:
        blocks = [jnp.pad(jnp.concatenate(blocks, axis=0), ((0, -rows * len(blocks) % 8), (0, 0)))]
    count = len(blocks)
    tile = tile_of(width)
    total = sum(block.shape[0] for block in blocks)
    return pl.pallas_call(
        functools.partial(flows_kernel, count),
        grid=(width // tile,),
        in_specs=[pl.BlockSpec((block.shape[0], tile), lambda i: (0, i)) for block in blocks]
        + [pl.BlockSpec((branches, tile), lambda i: (0, i))],
        out_specs=pl.BlockSpec((total, branches), lambda i: (0, 0)),
        out_shape=jax.ShapeDtypeStruct((total, branches), jnp.float32),
        compiler_params=LARGE,
        cost_estimate=FREE,
        name="flows",
    )(*blocks, ptdf)


def grad_flow_of(flows, limit, price):
    upper = jax.nn.sigmoid((flows - limit) / SMOOTH)
    lower = jax.nn.sigmoid((-flows - limit) / SMOOTH)
    return (price * (upper - lower)).astype(jnp.bfloat16)


def grads_kernel(rows, mine_ref, other_ref, limit_ref, price_ref, ptdf_ref, *out_refs):
    grad_flow = grad_flow_of(mine_ref[...] + other_ref[...], limit_ref[...], price_ref[...])
    part = jnp.dot(grad_flow, ptdf_ref[...], preferred_element_type=jnp.float32)
    for index, out_ref in enumerate(out_refs):
        out_ref[...] = part[index * rows : (index + 1) * rows].astype(out_ref.dtype)


def grads_of(mine, other, limit, price, ptdf, rows, types):
    branches, width = ptdf.shape
    if rows % 8:
        part = jnp.dot(grad_flow_of(mine + other, limit, price), ptdf, preferred_element_type=jnp.float32)
        return [part[i * rows : (i + 1) * rows] for i in range(len(types))]
    tile = tile_of(width)
    flow_spec = pl.BlockSpec(mine.shape, lambda i: (0, 0))
    class_spec = pl.BlockSpec((1, branches), lambda i: (0, 0))
    return pl.pallas_call(
        functools.partial(grads_kernel, rows),
        grid=(width // tile,),
        in_specs=[flow_spec, flow_spec, class_spec, class_spec, pl.BlockSpec((branches, tile), lambda i: (0, i))],
        out_specs=[pl.BlockSpec((rows, tile), lambda i: (0, i)) for _ in types],
        out_shape=[jax.ShapeDtypeStruct((rows, width), dtype) for dtype in types],
        compiler_params=LARGE,
        cost_estimate=FREE,
        name="grads",
    )(mine, other, limit, price, ptdf)


def pick_kernel(bus_ref, grad_ref, plant_ref, out_ref):
    rows, width = grad_ref.shape
    groups = width // 128
    column = plant_ref[...]
    place = column // 128 - (bus_ref[0] * pl.num_programs(0) + pl.program_id(0)) * groups
    lanes = scatter_lanes(column)
    stacked = jnp.concatenate([grad_ref[:, g * 128 : (g + 1) * 128] for g in range(groups)], axis=0)
    high, low = split_high(stacked)
    found = jnp.dot(
        jnp.concatenate([high, low], axis=1),
        jnp.concatenate([lanes, lanes], axis=0),
        preferred_element_type=jnp.float32,
    )
    total = jnp.zeros(out_ref.shape, jnp.float32)
    for group in range(groups):
        total += jnp.where(place == group, found[group * rows : (group + 1) * rows], 0.0)

    @pl.when(pl.program_id(0) == 0)
    def _():
        out_ref[...] = jnp.zeros_like(out_ref)

    out_ref[...] += total


def pick_of(bus, grad, plant_bus):
    rows, width = grad.shape
    short = -rows % 8
    if short:
        grad = jnp.pad(grad, ((0, short), (0, 0)))
    tile = tile_of(width)
    plants = plant_bus.shape[0]
    out = pl.pallas_call(
        pick_kernel,
        grid=(width // tile,),
        in_specs=[
            pl.BlockSpec(memory_space=pltpu.SMEM),
            pl.BlockSpec((rows + short, tile), lambda i: (0, i)),
            pl.BlockSpec((1, plants), lambda i: (0, 0)),
        ],
        out_specs=pl.BlockSpec((rows + short, plants), lambda i: (0, 0)),
        out_shape=jax.ShapeDtypeStruct((rows + short, plants), jnp.float32),
        compiler_params=LARGE,
        cost_estimate=FREE,
        name="pick",
    )(bus, grad, plant_bus[None, :])
    return out[:rows] if short else out


def make_shards(box, buses):
    gather, reduce, ends = plan(box)
    own = (0, 0, 0)

    def shards(net_load, release, plant_bus, efficiency, ptdf, branch_class, class_limit, class_price):
        rows = net_load.shape[0]
        bus = lax.axis_index("bus").astype(jnp.int32)[None]
        inject = inject_of(bus, net_load, release, efficiency, plant_bus)
        onehot = (branch_class[:, None] == jnp.arange(class_limit.shape[0])[None, :]).astype(jnp.float32)
        limit = jnp.sum(onehot * class_limit[None, :], axis=1)[None, :]
        price = jnp.sum(onehot * class_price[None, :], axis=1)[None, :]

        def over_bus(value):
            if buses == 2:
                return value, lax.ppermute(value, "bus", [(0, 1), (1, 0)])
            return lax.psum(value, "bus"), jnp.zeros_like(value)

        targets = {step_back(label, axis, shift, box) for now in reduce for axis, shift, label in now}

        def flows_now(labels):
            return over_bus(flows_of([have[label] for label in labels], ptdf))

        def grads_now(labels, flows):
            types = [jnp.float32 if label in targets else jnp.bfloat16 for label in labels]
            parts.update(zip(labels, grads_of(*flows, limit, price, ptdf, rows, types)))

        have, parts, fresh, last = {own: inject}, {}, [own], {}
        marks = {}
        for index, now in enumerate(gather):
            for axis, shift, label in now:
                block = after(have[step_back(label, axis, shift, box)], last.get(axis))
                block = after(block, marks.pop(index, None))
                have[label] = last[axis] = lax.ppermute(block, "br", moves(axis, shift, box))
                fresh.append(label)
            if index in ends:
                flows = flows_now(fresh)
                grads_now(fresh, flows)
                marks[index + 2] = flows[0]
                fresh = []

        for index, now in enumerate(reversed(reduce), len(gather)):
            for axis, shift, label in reversed(now):
                block = after(parts[label].astype(jnp.bfloat16), last.get(axis))
                block = after(block, marks.pop(index, None))
                last[axis] = lax.ppermute(block, "br", moves(axis, -shift, box))
                to = step_back(label, axis, shift, box)
                parts[to] = parts[to] + last[axis].astype(jnp.float32)
        grad_bus = parts[own]
        mine, other = over_bus(pick_of(bus, grad_bus, plant_bus))
        grad_release = (mine + other) * efficiency[None, :]
        return (grad_bus, grad_release)

    return shards


def solution(mesh):
    placed = (P("br", "bus"), P("br", None), P(), P(), P("br", "bus"), P("br"), P(), P())
    return jax.shard_map(
        make_shards(chip_box(mesh.shape["br"]), mesh.shape["bus"]),
        mesh=mesh,
        in_specs=placed,
        out_specs=(P("br", "bus"), P("br", None)),
        check_vma=False,
    )
```

```python
import functools

import jax
import jax.numpy as jnp
from jax import lax
from jax.experimental import pallas as pl
from jax.experimental.pallas import tpu as pltpu
from jax.sharding import PartitionSpec as P

SMOOTH = 0.25
Z, Y, X = 0, 1, 2
GATHER, REDUCE, FLOWS, GRADS = 0, 1, 2, 3


def chip_box(count):
    bits = (count // 2).bit_length() - 1
    nx = 1 << (bits // 2)
    return count // (2 * nx), 2, nx


PLAN = [
    (GATHER, Z, -1, (-1, 0, 0), ()),
    (GATHER, X, 1, (0, 0, 1), ()),
    (GATHER, Y, 1, (0, 1, 0), ()),
    (GATHER, Z, -1, (2, 0, 0), (0,)),
    (GATHER, X, 1, (-1, 0, 1), (1,)),
    (GATHER, Y, 1, (0, 1, 1), (2,)),
    (GATHER, Z, 1, (1, 1, 0), (3,)),
    (GATHER, X, 1, (2, 0, 1), (4,)),
    (GATHER, Y, 1, (-1, 1, 1), (5,)),
    (FLOWS, 0, [(0, 0, 0), (-1, 0, 0), (0, 0, 1), (0, 1, 0), (2, 0, 0), (-1, 0, 1), (0, 1, 1), (1, 1, 0), (2, 0, 1), (-1, 1, 1)], ()),
    (GRADS, 0),
    (GATHER, Z, 1, (1, 0, 0), (6,)),
    (GATHER, X, 1, (1, 1, 1), (7,)),
    (GATHER, Y, 1, (2, 1, 1), (8,)),
    (FLOWS, 1, [(1, 0, 0), (1, 1, 1), (2, 1, 1)], ()),
    (GRADS, 1),
    (GATHER, Z, 1, (2, 1, 0), (9, 11)),
    (GATHER, X, 1, (1, 0, 1), (9, 12)),
    (GATHER, Y, 1, (-1, 1, 0), (9, 13)),
    (FLOWS, 2, [(2, 1, 0), (1, 0, 1), (-1, 1, 0)], ()),
    (GRADS, 2),
    (REDUCE, Y, 1, (0, 1, 1), (14, 18)),
    (REDUCE, X, 1, (-1, 1, 1), (14, 17)),
    (REDUCE, Z, -1, (-1, 0, 1), (14, 16)),
    (REDUCE, Y, 1, (2, 1, 1), (19, 21)),
    (REDUCE, X, 1, (1, 1, 1), (19, 22)),
    (REDUCE, Z, -1, (-1, 0, 0), (19, 23)),
    (REDUCE, Y, 1, (2, 1, 0), (24,)),
    (REDUCE, X, 1, (2, 0, 1), (25,)),
    (REDUCE, Z, -1, (-1, 1, 0), (26,)),
    (REDUCE, Y, 1, (1, 1, 0), (27,)),
    (REDUCE, X, 1, (1, 0, 1), (28,)),
    (REDUCE, Z, 1, (2, 0, 0), (29,)),
    (REDUCE, Y, 1, (0, 1, 0), (30,)),
    (REDUCE, X, 1, (0, 0, 1), (31,)),
    (REDUCE, Z, 1, (1, 0, 0), (32,)),
]


def greedy(box):
    labels = [(z, y, x) for z in range(box[0]) for y in range(box[1]) for x in range(box[2])]
    have, sends = {(0, 0, 0)}, []
    while len(have) < len(labels):
        taken = set()
        for axis in (Z, X, Y):
            shifts = (1, -1) if box[axis] > 2 else (1,)
            options = [
                (shift, label)
                for label in labels
                if label not in have and label not in taken
                for shift in shifts
                if step_back(label, axis, shift, box) in have
            ]
            if options:
                shift, label = options[0]
                sends.append((axis, shift, label))
                taken.add(label)
        have |= taken
    return sends


def step_back(label, axis, shift, box):
    moved = list(label)
    moved[axis] = (moved[axis] - shift) % box[axis]
    return tuple(moved)


def plan(box):
    if box == (4, 2, 2):
        wrap = lambda label: tuple(c % n for c, n in zip(label, box))
        steps = []
        for step in PLAN:
            if step[0] in (GATHER, REDUCE):
                step = (*step[:3], wrap(step[3]), step[4])
            elif step[0] == FLOWS:
                step = (*step[:2], [wrap(label) for label in step[2]], step[3])
            steps.append(step)
        return steps
    sends = greedy(box)
    steps = [(GATHER, *send, ()) for send in sends]
    steps += [(FLOWS, 0, [(0, 0, 0)] + [label for _, _, label in sends], ()), (GRADS, 0)]
    return steps + [(REDUCE, *send, ()) for send in reversed(sends)]


def moves(axis, shift, box):
    pairs = []
    for z in range(box[0]):
        for y in range(box[1]):
            for x in range(box[2]):
                to = step_back((z, y, x), axis, -shift, box)
                pairs.append(((z * box[1] + y) * box[2] + x, (to[0] * box[1] + to[1]) * box[2] + to[2]))
    return pairs


def after(value, earlier):
    if not earlier:
        return value
    return lax.optimization_barrier((value, *earlier))[0]


SPLIT = 1


def tile_of(width):
    groups = width // 128
    return 128 * max(n for n in range(1, 65) if groups % n == 0)


def part_specs(rows, width):
    tile = tile_of(width // SPLIT)
    steps = width // SPLIT // tile
    return steps, tile, [pl.BlockSpec((rows, tile), lambda i, h=h: (0, h * steps + i)) for h in range(SPLIT)]


def scatter_lanes(column):
    lane = lax.broadcasted_iota(jnp.int32, (128, column.shape[1]), 0)
    return jnp.where(lane == column % 128, 1.0, 0.0).astype(jnp.bfloat16)


def split_high(value):
    high = value.astype(jnp.bfloat16)
    return high, (value - high.astype(jnp.float32)).astype(jnp.bfloat16)


def place_of(bus_ref, column, part, groups):
    tile = (bus_ref[0] * SPLIT + part) * pl.num_programs(0) + pl.program_id(0)
    return column // 128 - tile * groups


def inject_kernel(bus_ref, release_ref, efficiency_ref, plant_ref, *refs):
    net_refs, out_refs = refs[:SPLIT], refs[SPLIT:]
    rows, width = net_refs[0].shape
    groups = width // 128
    column = plant_ref[...]
    lanes = scatter_lanes(column)
    high, low = split_high(release_ref[...] * efficiency_ref[...])

    for part in range(SPLIT):
        place = place_of(bus_ref, column, part, groups)

        def spread(values):
            picked = [jnp.where(place == group, values, 0.0) for group in range(groups)]
            return lax.dot_general(
                jnp.concatenate(picked, axis=0).astype(jnp.bfloat16),
                lanes,
                (((1,), (1,)), ((), ())),
                preferred_element_type=jnp.float32,
            )

        added = spread(high.astype(jnp.float32)) + spread(low.astype(jnp.float32))
        for group in range(groups):
            at = slice(group * 128, (group + 1) * 128)
            total = net_refs[part][:, at].astype(jnp.float32) + added[group * rows : (group + 1) * rows]
            out_refs[part][:, at] = total.astype(jnp.bfloat16)


FREE = pl.CostEstimate(flops=0, bytes_accessed=0, transcendentals=0)


def vmem(mebibytes):
    return pltpu.CompilerParams(vmem_limit_bytes=mebibytes << 20)


def inject_of(bus, net_load, release, efficiency, plant_bus):
    rows, width = net_load.shape
    short = -rows % 8
    if short:
        net_load = jnp.pad(net_load, ((0, short), (0, 0)))
        release = jnp.pad(release, ((0, short), (0, 0)))
    steps, tile, specs = part_specs(rows + short, width)
    plants = release.shape[1]
    whole = pl.BlockSpec((1, plants), lambda i: (0, 0))
    outs = pl.pallas_call(
        inject_kernel,
        grid=(steps,),
        in_specs=[
            pl.BlockSpec(memory_space=pltpu.SMEM),
            pl.BlockSpec((rows + short, plants), lambda i: (0, 0)),
            whole,
            whole,
            *specs,
        ],
        out_specs=[pl.BlockSpec((rows + short, tile), lambda i: (0, i))] * SPLIT,
        out_shape=[jax.ShapeDtypeStruct((rows + short, width // SPLIT), jnp.bfloat16)] * SPLIT,
        compiler_params=vmem(60),
        cost_estimate=FREE,
        name="inject",
    )(bus, release, efficiency[None, :], plant_bus[None, :], *[net_load] * SPLIT)
    return [out[:rows] if short else out for out in outs]


def flows_kernel(count, *refs):
    blocks, ptdf_refs, out_ref = refs[: count * SPLIT], refs[count * SPLIT : -1], refs[-1]

    @pl.when(pl.program_id(0) == 0)
    def _():
        out_ref[...] = jnp.zeros_like(out_ref)

    total = out_ref[...]
    for part in range(SPLIT):
        rows = jnp.concatenate([block[...].astype(jnp.float32) for block in blocks[part::SPLIT]], axis=0)
        total += lax.dot_general(
            rows.astype(jnp.bfloat16),
            ptdf_refs[part][...],
            (((1,), (1,)), ((), ())),
            preferred_element_type=jnp.float32,
        )
    out_ref[...] = total


def flows_of(blocks, ptdf):
    rows = blocks[0][0].shape[0]
    branches, width = ptdf.shape
    if rows % 8:
        short = -rows * len(blocks) % 8
        blocks = [[jnp.pad(jnp.concatenate(part, axis=0), ((0, short), (0, 0))) for part in zip(*blocks)]]
        rows = blocks[0][0].shape[0]
    count = len(blocks)
    steps, tile, ptdf_specs = part_specs(branches, width)
    return pl.pallas_call(
        functools.partial(flows_kernel, count),
        grid=(steps,),
        in_specs=[pl.BlockSpec((rows, tile), lambda i: (0, i))] * (count * SPLIT) + ptdf_specs,
        out_specs=pl.BlockSpec((count * rows, branches), lambda i: (0, 0)),
        out_shape=jax.ShapeDtypeStruct((count * rows, branches), jnp.float32),
        compiler_params=vmem(24),
        cost_estimate=FREE,
        name="flows",
    )(*[part for block in blocks for part in block], *[ptdf] * SPLIT)


def grad_flow_of(flows, limit, price):
    upper = jax.nn.sigmoid((flows - limit) / SMOOTH)
    lower = jax.nn.sigmoid((-flows - limit) / SMOOTH)
    return (price * (upper - lower)).astype(jnp.bfloat16)


def grads_kernel(rows, mine_ref, other_ref, limit_ref, price_ref, *refs):
    ptdf_refs, out_refs = refs[:SPLIT], refs[SPLIT:]
    grad_flow = grad_flow_of(mine_ref[...] + other_ref[...], limit_ref[...], price_ref[...])
    for part in range(SPLIT):
        grads = jnp.dot(grad_flow, ptdf_refs[part][...], preferred_element_type=jnp.float32)
        for index, out_ref in enumerate(out_refs[part::SPLIT]):
            out_ref[...] = grads[index * rows : (index + 1) * rows].astype(out_ref.dtype)


def grads_of(mine, other, limit, price, ptdf, rows, types):
    branches, width = ptdf.shape
    if rows % 8:
        grads = jnp.dot(grad_flow_of(mine + other, limit, price), ptdf, preferred_element_type=jnp.float32)
        return [jnp.split(grads[i * rows : (i + 1) * rows], SPLIT, axis=1) for i in range(len(types))]
    steps, tile, ptdf_specs = part_specs(branches, width)
    flow_spec = pl.BlockSpec(mine.shape, lambda i: (0, 0))
    class_spec = pl.BlockSpec((1, branches), lambda i: (0, 0))
    outs = pl.pallas_call(
        functools.partial(grads_kernel, rows),
        grid=(steps,),
        in_specs=[flow_spec, flow_spec, class_spec, class_spec, *ptdf_specs],
        out_specs=[pl.BlockSpec((rows, tile), lambda i: (0, i))] * (len(types) * SPLIT),
        out_shape=[jax.ShapeDtypeStruct((rows, width // SPLIT), dtype) for dtype in types for _ in range(SPLIT)],
        compiler_params=vmem(32),
        cost_estimate=FREE,
        name="grads",
    )(mine, other, limit, price, *[ptdf] * SPLIT)
    return [outs[i * SPLIT : (i + 1) * SPLIT] for i in range(len(types))]


def finish_kernel(terms, bus_ref, plant_ref, *refs):
    grad_ref, found_ref = refs[-2:]
    rows, half = refs[0].shape
    groups = half // 128
    column = plant_ref[...]
    lanes = scatter_lanes(column)
    lanes = jnp.concatenate([lanes, lanes], axis=0)
    picked = jnp.zeros(found_ref.shape, jnp.float32)
    for part in range(SPLIT):
        grad = refs[part][...]
        for term in range(1, terms):
            grad += refs[term * SPLIT + part][...].astype(jnp.float32)
        grad_ref[:, part * half : (part + 1) * half] = grad
        place = place_of(bus_ref, column, part, groups)
        high, low = split_high(jnp.concatenate([grad[:, g * 128 : (g + 1) * 128] for g in range(groups)], axis=0))
        found = jnp.dot(jnp.concatenate([high, low], axis=1), lanes, preferred_element_type=jnp.float32)
        for group in range(groups):
            picked += jnp.where(place == group, found[group * rows : (group + 1) * rows], 0.0)
    found_ref[...] = picked


def finish_of(bus, plant_bus, terms):
    rows, half = terms[0][0].shape
    short = -rows % 8
    if short:
        terms = [[jnp.pad(part, ((0, short), (0, 0))) for part in term] for term in terms]
    plants = plant_bus.shape[0]
    grad, found = pl.pallas_call(
        functools.partial(finish_kernel, len(terms)),
        grid=(1,),
        in_specs=[pl.BlockSpec(memory_space=pltpu.SMEM), pl.BlockSpec((1, plants), lambda i: (0, 0))]
        + [pl.BlockSpec((rows + short, half), lambda i: (0, 0))] * (len(terms) * SPLIT),
        out_specs=[
            pl.BlockSpec((rows + short, SPLIT * half), lambda i: (0, 0)),
            pl.BlockSpec((rows + short, plants), lambda i: (0, 0)),
        ],
        out_shape=[
            jax.ShapeDtypeStruct((rows + short, SPLIT * half), jnp.float32),
            jax.ShapeDtypeStruct((rows + short, plants), jnp.float32),
        ],
        compiler_params=vmem(48),
        cost_estimate=FREE,
        name="finish",
    )(bus, plant_bus[None, :], *[part for term in terms for part in term])
    return (grad[:rows], found[:rows]) if short else (grad, found)


def total_of(terms):
    totals = []
    for part, *more in zip(*terms):
        for term in more:
            part = part + term.astype(jnp.float32)
        totals.append(part.astype(jnp.bfloat16))
    return totals


def make_shards(box, buses):
    steps = plan(box)
    targets = {step_back(step[3], step[1], step[2], box) for step in steps if step[0] == REDUCE}
    own = (0, 0, 0)

    def shards(net_load, release, plant_bus, efficiency, ptdf, branch_class, class_limit, class_price):
        rows = net_load.shape[0]
        bus = lax.axis_index("bus").astype(jnp.int32)[None]
        inject = inject_of(bus, net_load, release, efficiency, plant_bus)
        onehot = (branch_class[:, None] == jnp.arange(class_limit.shape[0])[None, :]).astype(jnp.float32)
        limit = jnp.sum(onehot * class_limit[None, :], axis=1)[None, :]
        price = jnp.sum(onehot * class_price[None, :], axis=1)[None, :]

        def over_bus(value):
            if buses == 2:
                return value, lax.ppermute(value, "bus", [(0, 1), (1, 0)])
            return lax.psum(value, "bus"), jnp.zeros_like(value)

        have, terms, flows, over = {own: inject}, {}, {}, []
        for step in steps:
            if step[0] == FLOWS:
                _, batch, labels, waits = step
                blocks = [have[label] for label in labels]
                blocks[-1] = [after(part, [over[i] for i in waits]) for part in blocks[-1]]
                flows[batch] = labels, over_bus(flows_of(blocks, ptdf))
                over.append(flows[batch][1][0])
            elif step[0] == GRADS:
                labels, sides = flows[step[1]]
                types = [jnp.float32 if label in targets else jnp.bfloat16 for label in labels]
                parts = grads_of(*sides, limit, price, ptdf, rows, types)
                terms.update((label, [part]) for label, part in zip(labels, parts))
                over.append(parts[0][0])
            else:
                kind, axis, shift, label, waits = step
                near = step_back(label, axis, shift, box)
                block = have[near] if kind == GATHER else total_of(terms[label])
                waits = [over[i] for i in waits]
                pairs = moves(axis, shift if kind == GATHER else -shift, box)
                with jax.named_scope(f"send_{len(over)}"):
                    came = [lax.ppermute(after(part, waits), "br", pairs) for part in block]
                if kind == GATHER:
                    have[label] = came
                else:
                    terms[near].append(came)
                over.append(came[-1])
        grad_bus, found = finish_of(bus, plant_bus, terms[own])
        mine, other = over_bus(found)
        grad_release = (mine + other) * efficiency[None, :]
        return (grad_bus, grad_release)

    return shards


def solution(mesh):
    placed = (P("br", "bus"), P("br", None), P(), P(), P("br", "bus"), P("br"), P(), P())
    return jax.shard_map(
        make_shards(chip_box(mesh.shape["br"]), mesh.shape["bus"]),
        mesh=mesh,
        in_specs=placed,
        out_specs=(P("br", "bus"), P("br", None)),
        check_vma=False,
    )
```

```python
import functools

import jax
import jax.numpy as jnp
from jax import lax
from jax.experimental import pallas as pl
from jax.experimental.pallas import tpu as pltpu
from jax.sharding import PartitionSpec as P

SMOOTH = 0.25
Z, Y, X = 0, 1, 2
GATHER, REDUCE, FLOWS, GRADS = 0, 1, 2, 3


def chip_box(count):
    bits = (count // 2).bit_length() - 1
    nx = 1 << (bits // 2)
    return count // (2 * nx), 2, nx


PLAN = [
    (GATHER, Z, -1, (-1, 0, 0), ()),
    (GATHER, X, 1, (0, 0, 1), ()),
    (GATHER, Y, 1, (0, 1, 0), ()),
    (GATHER, Z, -1, (2, 0, 0), (0,)),
    (GATHER, X, 1, (-1, 0, 1), (1,)),
    (GATHER, Y, 1, (0, 1, 1), (2,)),
    (GATHER, Z, 1, (1, 1, 0), (3,)),
    (GATHER, X, 1, (2, 0, 1), (4,)),
    (GATHER, Y, 1, (-1, 1, 1), (5,)),
    (FLOWS, 0, [(0, 0, 0), (-1, 0, 0), (0, 0, 1), (0, 1, 0), (2, 0, 0), (-1, 0, 1), (0, 1, 1), (1, 1, 0), (2, 0, 1), (-1, 1, 1)], ()),
    (GRADS, 0),
    (GATHER, Z, 1, (1, 0, 0), (6,)),
    (GATHER, X, 1, (1, 1, 1), (7,)),
    (GATHER, Y, 1, (2, 1, 1), (8,)),
    (GATHER, Z, 1, (2, 1, 0), (9, 11)),
    (GATHER, X, 1, (1, 0, 1), (9, 12)),
    (GATHER, Y, 1, (-1, 1, 0), (9, 13)),
    (FLOWS, 1, [(1, 0, 0), (1, 1, 1), (2, 1, 1), (2, 1, 0), (1, 0, 1), (-1, 1, 0)], ()),
    (GRADS, 1),
    (REDUCE, Y, 1, (0, 1, 1), (16,)),
    (REDUCE, X, 1, (-1, 1, 1), (15,)),
    (REDUCE, Z, -1, (-1, 0, 1), (14,)),
    (REDUCE, Y, 1, (2, 1, 1), (17, 19)),
    (REDUCE, X, 1, (1, 1, 1), (17, 20)),
    (REDUCE, Z, -1, (-1, 0, 0), (17, 21)),
    (REDUCE, Y, 1, (2, 1, 0), (22,)),
    (REDUCE, X, 1, (2, 0, 1), (23,)),
    (REDUCE, Z, -1, (-1, 1, 0), (24,)),
    (REDUCE, Y, 1, (1, 1, 0), (25,)),
    (REDUCE, X, 1, (1, 0, 1), (26,)),
    (REDUCE, Z, 1, (2, 0, 0), (27,)),
    (REDUCE, Y, 1, (0, 1, 0), (28,)),
    (REDUCE, X, 1, (0, 0, 1), (29,)),
    (REDUCE, Z, 1, (1, 0, 0), (30,)),
]


def greedy(box):
    labels = [(z, y, x) for z in range(box[0]) for y in range(box[1]) for x in range(box[2])]
    have, sends = {(0, 0, 0)}, []
    while len(have) < len(labels):
        taken = set()
        for axis in (Z, X, Y):
            shifts = (1, -1) if box[axis] > 2 else (1,)
            options = [
                (shift, label)
                for label in labels
                if label not in have and label not in taken
                for shift in shifts
                if step_back(label, axis, shift, box) in have
            ]
            if options:
                shift, label = options[0]
                sends.append((axis, shift, label))
                taken.add(label)
        have |= taken
    return sends


def step_back(label, axis, shift, box):
    moved = list(label)
    moved[axis] = (moved[axis] - shift) % box[axis]
    return tuple(moved)


def plan(box):
    if box == (4, 2, 2):
        wrap = lambda label: tuple(c % n for c, n in zip(label, box))
        steps = []
        for step in PLAN:
            if step[0] in (GATHER, REDUCE):
                step = (*step[:3], wrap(step[3]), step[4])
            elif step[0] == FLOWS:
                step = (*step[:2], [wrap(label) for label in step[2]], step[3])
            steps.append(step)
        return steps
    sends = greedy(box)
    steps = [(GATHER, *send, ()) for send in sends]
    steps += [(FLOWS, 0, [(0, 0, 0)] + [label for _, _, label in sends], ()), (GRADS, 0)]
    return steps + [(REDUCE, *send, ()) for send in reversed(sends)]


def moves(axis, shift, box):
    pairs = []
    for z in range(box[0]):
        for y in range(box[1]):
            for x in range(box[2]):
                to = step_back((z, y, x), axis, -shift, box)
                pairs.append(((z * box[1] + y) * box[2] + x, (to[0] * box[1] + to[1]) * box[2] + to[2]))
    return pairs


def after(value, earlier):
    if not earlier:
        return value
    return lax.optimization_barrier((value, *earlier))[0]


def tile_of(width, group):
    groups = width // group
    return group * max(n for n in range(1, 65) if groups % n == 0)


GROUP = 256


def scatter_lanes(column):
    lane = lax.broadcasted_iota(jnp.int32, (GROUP, column.shape[1]), 0)
    return jnp.where(lane == column % GROUP, 1.0, 0.0).astype(jnp.bfloat16)


def split_high(value):
    high = value.astype(jnp.bfloat16)
    return high, (value - high.astype(jnp.float32)).astype(jnp.bfloat16)


def place_of(bus_ref, column, groups):
    tile = bus_ref[0] * pl.num_programs(0) + pl.program_id(0)
    return column // GROUP - tile * groups


def inject_kernel(bus_ref, release_ref, efficiency_ref, plant_ref, net_ref, out_ref):
    rows, width = net_ref.shape
    groups = width // GROUP
    column = plant_ref[...]
    lanes = scatter_lanes(column)
    place = place_of(bus_ref, column, groups)

    def spread(values):
        picked = [jnp.where(place == group, values, 0.0) for group in range(groups)]
        return lax.dot_general(
            jnp.concatenate(picked, axis=0).astype(jnp.bfloat16),
            lanes,
            (((1,), (1,)), ((), ())),
            preferred_element_type=jnp.float32,
        )

    high, low = split_high(release_ref[...] * efficiency_ref[...])
    added = spread(high.astype(jnp.float32)) + spread(low.astype(jnp.float32))
    for group in range(groups):
        at = slice(group * GROUP, (group + 1) * GROUP)
        total = net_ref[:, at].astype(jnp.float32) + added[group * rows : (group + 1) * rows]
        out_ref[:, at] = total.astype(jnp.bfloat16)


FREE = pl.CostEstimate(flops=0, bytes_accessed=0, transcendentals=0)


def vmem(mebibytes):
    return pltpu.CompilerParams(vmem_limit_bytes=mebibytes << 20)


def inject_of(bus, net_load, release, efficiency, plant_bus):
    rows, width = net_load.shape
    short = -rows % 8
    if short:
        net_load = jnp.pad(net_load, ((0, short), (0, 0)))
        release = jnp.pad(release, ((0, short), (0, 0)))
    tile = tile_of(width, GROUP)
    plants = release.shape[1]
    whole = pl.BlockSpec((1, plants), lambda i: (0, 0))
    tiled = pl.BlockSpec((rows + short, tile), lambda i: (0, i))
    out = pl.pallas_call(
        inject_kernel,
        grid=(width // tile,),
        in_specs=[
            pl.BlockSpec(memory_space=pltpu.SMEM),
            pl.BlockSpec((rows + short, plants), lambda i: (0, 0)),
            whole,
            whole,
            tiled,
        ],
        out_specs=tiled,
        out_shape=jax.ShapeDtypeStruct(net_load.shape, jnp.bfloat16),
        compiler_params=vmem(60),
        cost_estimate=FREE,
        name="inject",
    )(bus, release, efficiency[None, :], plant_bus[None, :], net_load)
    return out[:rows] if short else out


RESIDENT = pl.BlockSpec(memory_space=pltpu.VMEM)


def flows_kernel(tile, *refs):
    *blocks, ptdf_ref, out_ref = refs
    total = jnp.zeros(out_ref.shape, jnp.float32)

    def add(i, total):
        at = pl.ds(pl.multiple_of(i * tile, 128), tile)
        rows = jnp.concatenate([block[:, at].astype(jnp.float32) for block in blocks], axis=0)
        return total + lax.dot_general(
            rows.astype(jnp.bfloat16), ptdf_ref[:, at], (((1,), (1,)), ((), ())), preferred_element_type=jnp.float32
        )

    out_ref[...] = lax.fori_loop(0, ptdf_ref.shape[1] // tile, add, total)


def flows_of(blocks, ptdf):
    rows = blocks[0].shape[0]
    branches, width = ptdf.shape
    if rows % 8:
        short = -rows * len(blocks) % 8
        blocks = [jnp.pad(jnp.concatenate(blocks, axis=0), ((0, short), (0, 0)))]
        rows = blocks[0].shape[0]
    count = len(blocks)
    return pl.pallas_call(
        functools.partial(flows_kernel, tile_of(width, 128)),
        in_specs=[RESIDENT] * (count + 1),
        out_specs=RESIDENT,
        out_shape=jax.ShapeDtypeStruct((count * rows, branches), jnp.float32),
        compiler_params=vmem(16),
        cost_estimate=FREE,
        name="flows",
    )(*blocks, ptdf)


def grad_flow_of(flows, limit, price):
    upper = jax.nn.sigmoid((flows - limit) / SMOOTH)
    lower = jax.nn.sigmoid((-flows - limit) / SMOOTH)
    return (price * (upper - lower)).astype(jnp.bfloat16)


def grads_kernel(tile, mine_ref, other_ref, limit_ref, price_ref, ptdf_ref, *out_refs):
    rows = out_refs[0].shape[0]
    grad_flow = grad_flow_of(mine_ref[...] + other_ref[...], limit_ref[...], price_ref[...])

    @pl.loop(0, ptdf_ref.shape[1] // tile)
    def _(i):
        at = pl.ds(pl.multiple_of(i * tile, 128), tile)
        grads = jnp.dot(grad_flow, ptdf_ref[:, at], preferred_element_type=jnp.float32)
        for index, out_ref in enumerate(out_refs):
            out_ref[:, at] = grads[index * rows : (index + 1) * rows].astype(out_ref.dtype)


def grads_of(mine, other, limit, price, ptdf, rows, types):
    width = ptdf.shape[1]
    if rows % 8:
        grads = jnp.dot(grad_flow_of(mine + other, limit, price), ptdf, preferred_element_type=jnp.float32)
        return [grads[i * rows : (i + 1) * rows] for i in range(len(types))]
    return pl.pallas_call(
        functools.partial(grads_kernel, tile_of(width, 128)),
        in_specs=[RESIDENT] * 5,
        out_specs=[RESIDENT] * len(types),
        out_shape=[jax.ShapeDtypeStruct((rows, width), dtype) for dtype in types],
        compiler_params=vmem(16),
        cost_estimate=FREE,
        name="grads",
    )(mine, other, limit, price, ptdf)


def finish_kernel(bus_ref, plant_ref, *refs):
    *terms, grad_ref, found_ref = refs
    rows, width = grad_ref.shape
    groups = width // GROUP
    column = plant_ref[...]
    lanes = scatter_lanes(column)
    grad = sum(term[...].astype(jnp.float32) for term in terms)
    grad_ref[...] = grad
    place = place_of(bus_ref, column, groups)
    high, low = split_high(jnp.concatenate([grad[:, g * GROUP : (g + 1) * GROUP] for g in range(groups)], axis=0))
    found = jnp.dot(
        jnp.concatenate([high, low], axis=1),
        jnp.concatenate([lanes, lanes], axis=0),
        preferred_element_type=jnp.float32,
    )
    picked = jnp.zeros(found_ref.shape, jnp.float32)
    for group in range(groups):
        picked += jnp.where(place == group, found[group * rows : (group + 1) * rows], 0.0)
    found_ref[...] = picked


def finish_of(bus, plant_bus, terms):
    rows, width = terms[0].shape
    short = -rows % 8
    if short:
        terms = [jnp.pad(term, ((0, short), (0, 0))) for term in terms]
    plants = plant_bus.shape[0]
    whole = pl.BlockSpec((rows + short, width), lambda i: (0, 0))
    grad, found = pl.pallas_call(
        finish_kernel,
        grid=(1,),
        in_specs=[pl.BlockSpec(memory_space=pltpu.SMEM), pl.BlockSpec((1, plants), lambda i: (0, 0))]
        + [whole] * len(terms),
        out_specs=[whole, pl.BlockSpec((rows + short, plants), lambda i: (0, 0))],
        out_shape=[
            jax.ShapeDtypeStruct((rows + short, width), jnp.float32),
            jax.ShapeDtypeStruct((rows + short, plants), jnp.float32),
        ],
        compiler_params=vmem(48),
        cost_estimate=FREE,
        name="finish",
    )(bus, plant_bus[None, :], *terms)
    return (grad[:rows], found[:rows]) if short else (grad, found)


def total_of(terms):
    return sum(term.astype(jnp.float32) for term in terms).astype(jnp.bfloat16)


def make_shards(box, buses):
    steps = plan(box)
    targets = {step_back(step[3], step[1], step[2], box) for step in steps if step[0] == REDUCE}
    own = (0, 0, 0)

    def shards(net_load, release, plant_bus, efficiency, ptdf, branch_class, class_limit, class_price):
        rows = net_load.shape[0]
        bus = lax.axis_index("bus").astype(jnp.int32)[None]
        inject = inject_of(bus, net_load, release, efficiency, plant_bus)
        onehot = (branch_class[:, None] == jnp.arange(class_limit.shape[0])[None, :]).astype(jnp.float32)
        limit = jnp.sum(onehot * class_limit[None, :], axis=1)[None, :]
        price = jnp.sum(onehot * class_price[None, :], axis=1)[None, :]

        def over_bus(value):
            if buses == 2:
                return value, lax.ppermute(value, "bus", [(0, 1), (1, 0)])
            return lax.psum(value, "bus"), jnp.zeros_like(value)

        have, terms, flows, over = {own: inject}, {}, {}, []
        for step in steps:
            if step[0] == FLOWS:
                _, batch, labels, waits = step
                blocks = [have[label] for label in labels]
                blocks[-1] = after(blocks[-1], [over[i] for i in waits])
                flows[batch] = labels, over_bus(flows_of(blocks, ptdf))
                over.append(flows[batch][1][0])
            elif step[0] == GRADS:
                labels, sides = flows[step[1]]
                types = [jnp.float32 if label in targets else jnp.bfloat16 for label in labels]
                parts = grads_of(*sides, limit, price, ptdf, rows, types)
                terms.update((label, [part]) for label, part in zip(labels, parts))
                over.append(parts[0])
            else:
                kind, axis, shift, label, waits = step
                near = step_back(label, axis, shift, box)
                block = have[near] if kind == GATHER else total_of(terms[label])
                waits = [over[i] for i in waits]
                pairs = moves(axis, shift if kind == GATHER else -shift, box)
                with jax.named_scope(f"send_{len(over)}"):
                    came = lax.ppermute(after(block, waits), "br", pairs)
                if kind == GATHER:
                    have[label] = came
                else:
                    terms[near].append(came)
                over.append(came)
        grad_bus, found = finish_of(bus, plant_bus, terms[own])
        mine, other = over_bus(found)
        grad_release = (mine + other) * efficiency[None, :]
        return (grad_bus, grad_release)

    return shards


def solution(mesh):
    placed = (P("br", "bus"), P("br", None), P(), P(), P("br", "bus"), P("br"), P(), P())
    return jax.shard_map(
        make_shards(chip_box(mesh.shape["br"]), mesh.shape["bus"]),
        mesh=mesh,
        in_specs=placed,
        out_specs=(P("br", "bus"), P("br", None)),
        check_vma=False,
    )
```

```python
import functools

import jax
import jax.numpy as jnp
from jax import lax
from jax.experimental import pallas as pl
from jax.experimental.pallas import tpu as pltpu
from jax.sharding import PartitionSpec as P

SMOOTH = 0.25
Z, Y, X = 0, 1, 2
GATHER, REDUCE, FLOWS, GRADS = 0, 1, 2, 3


def chip_box(count):
    bits = (count // 2).bit_length() - 1
    nx = 1 << (bits // 2)
    return count // (2 * nx), 2, nx


PLAN = [
    (GATHER, Z, 1, (1, 0, 0), ()),
    (GATHER, X, 1, (0, 0, 1), ()),
    (GATHER, Y, 1, (0, 1, 0), ()),
    (GATHER, Z, 1, (2, 0, 0), (0,)),
    (GATHER, X, 1, (1, 0, 1), (1,)),
    (GATHER, Y, 1, (0, 1, 1), (2,)),
    (GATHER, Z, -1, (-1, 0, 1), (3,)),
    (GATHER, X, 1, (2, 0, 1), (4,)),
    (GATHER, Y, 1, (1, 1, 1), (5,)),
    (FLOWS, 0, [(0, 0, 0), (1, 0, 0), (0, 0, 1), (0, 1, 0), (2, 0, 0), (1, 0, 1), (0, 1, 1), (-1, 0, 1), (2, 0, 1), (1, 1, 1)], ()),
    (GRADS, 0),
    (GATHER, Z, -1, (-1, 1, 1), (6,)),
    (GATHER, X, 1, (-1, 0, 0), (7,)),
    (GATHER, Y, 1, (2, 1, 1), (8,)),
    (GATHER, Z, -1, (-1, 1, 0), (9, 11)),
    (GATHER, X, 1, (1, 1, 0), (9, 12)),
    (GATHER, Y, 1, (2, 1, 0), (9, 13)),
    (FLOWS, 1, [(-1, 1, 1), (-1, 0, 0), (2, 1, 1), (-1, 1, 0), (1, 1, 0), (2, 1, 0)], ()),
    (GRADS, 1),
    (REDUCE, Y, 1, (0, 1, 1), (16,)),
    (REDUCE, X, 1, (1, 1, 1), (15,)),
    (REDUCE, Z, 1, (1, 0, 0), (14,)),
    (REDUCE, Y, 1, (2, 1, 1), (17, 19)),
    (REDUCE, X, 1, (-1, 1, 1), (17, 20)),
    (REDUCE, Z, 1, (1, 0, 1), (17, 21)),
    (REDUCE, Y, 1, (2, 1, 0), (22,)),
    (REDUCE, X, 1, (2, 0, 1), (23,)),
    (REDUCE, Z, 1, (1, 1, 0), (24,)),
    (REDUCE, Y, 1, (-1, 1, 0), (25,)),
    (REDUCE, X, 1, (-1, 0, 1), (26,)),
    (REDUCE, Z, -1, (2, 0, 0), (27,)),
    (REDUCE, Y, 1, (0, 1, 0), (28,)),
    (REDUCE, X, 1, (0, 0, 1), (29,)),
    (REDUCE, Z, -1, (-1, 0, 0), (30,)),
]


def greedy(box):
    labels = [(z, y, x) for z in range(box[0]) for y in range(box[1]) for x in range(box[2])]
    have, sends = {(0, 0, 0)}, []
    while len(have) < len(labels):
        taken = set()
        for axis in (Z, X, Y):
            shifts = (1, -1) if box[axis] > 2 else (1,)
            options = [
                (shift, label)
                for label in labels
                if label not in have and label not in taken
                for shift in shifts
                if step_back(label, axis, shift, box) in have
            ]
            if options:
                shift, label = options[0]
                sends.append((axis, shift, label))
                taken.add(label)
        have |= taken
    return sends


def step_back(label, axis, shift, box):
    moved = list(label)
    moved[axis] = (moved[axis] - shift) % box[axis]
    return tuple(moved)


def plan(box):
    if box == (4, 2, 2):
        wrap = lambda label: tuple(c % n for c, n in zip(label, box))
        steps = []
        for step in PLAN:
            if step[0] in (GATHER, REDUCE):
                step = (*step[:3], wrap(step[3]), step[4])
            elif step[0] == FLOWS:
                step = (*step[:2], [wrap(label) for label in step[2]], step[3])
            steps.append(step)
        return steps
    sends = greedy(box)
    steps = [(GATHER, *send, ()) for send in sends]
    steps += [(FLOWS, 0, [(0, 0, 0)] + [label for _, _, label in sends], ()), (GRADS, 0)]
    return steps + [(REDUCE, *send, ()) for send in reversed(sends)]


def moves(axis, shift, box):
    pairs = []
    for z in range(box[0]):
        for y in range(box[1]):
            for x in range(box[2]):
                to = step_back((z, y, x), axis, -shift, box)
                pairs.append(((z * box[1] + y) * box[2] + x, (to[0] * box[1] + to[1]) * box[2] + to[2]))
    return pairs


def after(value, earlier):
    if not earlier:
        return value
    return lax.optimization_barrier((value, *earlier))[0]


def tile_of(width, group):
    groups = width // group
    return group * max(n for n in range(1, 65) if groups % n == 0)


GROUP = 256


def scatter_lanes(column):
    lane = lax.broadcasted_iota(jnp.int32, (GROUP, column.shape[1]), 0)
    return jnp.where(lane == column % GROUP, 1.0, 0.0).astype(jnp.bfloat16)


def split_high(value):
    high = value.astype(jnp.bfloat16)
    return high, (value - high.astype(jnp.float32)).astype(jnp.bfloat16)


def place_of(bus_ref, column, groups):
    tile = bus_ref[0] * pl.num_programs(0) + pl.program_id(0)
    return column // GROUP - tile * groups


def inject_kernel(bus_ref, release_ref, efficiency_ref, plant_ref, net_ref, out_ref):
    rows, width = net_ref.shape
    groups = width // GROUP
    column = plant_ref[...]
    lanes = scatter_lanes(column)
    place = place_of(bus_ref, column, groups)

    def spread(values):
        picked = [jnp.where(place == group, values, 0.0) for group in range(groups)]
        return lax.dot_general(
            jnp.concatenate(picked, axis=0).astype(jnp.bfloat16),
            lanes,
            (((1,), (1,)), ((), ())),
            preferred_element_type=jnp.float32,
        )

    high, low = split_high(release_ref[...] * efficiency_ref[...])
    added = spread(high.astype(jnp.float32)) + spread(low.astype(jnp.float32))
    for group in range(groups):
        at = slice(group * GROUP, (group + 1) * GROUP)
        total = net_ref[:, at].astype(jnp.float32) + added[group * rows : (group + 1) * rows]
        out_ref[:, at] = total.astype(jnp.bfloat16)


FREE = pl.CostEstimate(flops=0, bytes_accessed=0, transcendentals=0)


def vmem(mebibytes):
    return pltpu.CompilerParams(vmem_limit_bytes=mebibytes << 20)


def inject_of(bus, net_load, release, efficiency, plant_bus):
    rows, width = net_load.shape
    short = -rows % 8
    if short:
        net_load = jnp.pad(net_load, ((0, short), (0, 0)))
        release = jnp.pad(release, ((0, short), (0, 0)))
    tile = tile_of(width, GROUP)
    plants = release.shape[1]
    whole = pl.BlockSpec((1, plants), lambda i: (0, 0))
    tiled = pl.BlockSpec((rows + short, tile), lambda i: (0, i))
    out = pl.pallas_call(
        inject_kernel,
        grid=(width // tile,),
        in_specs=[
            pl.BlockSpec(memory_space=pltpu.SMEM),
            pl.BlockSpec((rows + short, plants), lambda i: (0, 0)),
            whole,
            whole,
            tiled,
        ],
        out_specs=tiled,
        out_shape=jax.ShapeDtypeStruct(net_load.shape, jnp.bfloat16),
        compiler_params=vmem(60),
        cost_estimate=FREE,
        name="inject",
    )(bus, release, efficiency[None, :], plant_bus[None, :], net_load)
    return out[:rows] if short else out


RESIDENT = pl.BlockSpec(memory_space=pltpu.VMEM)


def flows_kernel(tile, *refs):
    *blocks, ptdf_ref, out_ref = refs
    total = jnp.zeros(out_ref.shape, jnp.float32)

    def add(i, total):
        at = pl.ds(pl.multiple_of(i * tile, 128), tile)
        rows = jnp.concatenate([block[:, at].astype(jnp.float32) for block in blocks], axis=0)
        return total + lax.dot_general(
            rows.astype(jnp.bfloat16), ptdf_ref[:, at], (((1,), (1,)), ((), ())), preferred_element_type=jnp.float32
        )

    out_ref[...] = lax.fori_loop(0, ptdf_ref.shape[1] // tile, add, total)


def flows_of(blocks, ptdf):
    rows = blocks[0].shape[0]
    branches, width = ptdf.shape
    if rows % 8:
        short = -rows * len(blocks) % 8
        blocks = [jnp.pad(jnp.concatenate(blocks, axis=0), ((0, short), (0, 0)))]
        rows = blocks[0].shape[0]
    count = len(blocks)
    return pl.pallas_call(
        functools.partial(flows_kernel, tile_of(width, 128)),
        in_specs=[RESIDENT] * (count + 1),
        out_specs=RESIDENT,
        out_shape=jax.ShapeDtypeStruct((count * rows, branches), jnp.float32),
        compiler_params=vmem(16),
        cost_estimate=FREE,
        name="flows",
    )(*blocks, ptdf)


def grad_flow_of(flows, limit, price):
    upper = jax.nn.sigmoid((flows - limit) / SMOOTH)
    lower = jax.nn.sigmoid((-flows - limit) / SMOOTH)
    return (price * (upper - lower)).astype(jnp.bfloat16)


def grads_kernel(tile, mine_ref, other_ref, limit_ref, price_ref, ptdf_ref, *out_refs):
    rows = out_refs[0].shape[0]
    grad_flow = grad_flow_of(mine_ref[...] + other_ref[...], limit_ref[...], price_ref[...])

    @pl.loop(0, ptdf_ref.shape[1] // tile)
    def _(i):
        at = pl.ds(pl.multiple_of(i * tile, 128), tile)
        grads = jnp.dot(grad_flow, ptdf_ref[:, at], preferred_element_type=jnp.float32)
        for index, out_ref in enumerate(out_refs):
            out_ref[:, at] = grads[index * rows : (index + 1) * rows].astype(out_ref.dtype)


def grads_of(mine, other, limit, price, ptdf, rows, types):
    width = ptdf.shape[1]
    if rows % 8:
        grads = jnp.dot(grad_flow_of(mine + other, limit, price), ptdf, preferred_element_type=jnp.float32)
        return [grads[i * rows : (i + 1) * rows] for i in range(len(types))]
    return pl.pallas_call(
        functools.partial(grads_kernel, tile_of(width, 128)),
        in_specs=[RESIDENT] * 5,
        out_specs=[RESIDENT] * len(types),
        out_shape=[jax.ShapeDtypeStruct((rows, width), dtype) for dtype in types],
        compiler_params=vmem(16),
        cost_estimate=FREE,
        name="grads",
    )(mine, other, limit, price, ptdf)


def finish_kernel(bus_ref, plant_ref, *refs):
    *terms, grad_ref, found_ref = refs
    rows, width = grad_ref.shape
    groups = width // GROUP
    column = plant_ref[...]
    lanes = scatter_lanes(column)
    grad = sum(term[...].astype(jnp.float32) for term in terms)
    grad_ref[...] = grad
    place = place_of(bus_ref, column, groups)
    high, low = split_high(jnp.concatenate([grad[:, g * GROUP : (g + 1) * GROUP] for g in range(groups)], axis=0))
    found = jnp.dot(
        jnp.concatenate([high, low], axis=1),
        jnp.concatenate([lanes, lanes], axis=0),
        preferred_element_type=jnp.float32,
    )
    picked = jnp.zeros(found_ref.shape, jnp.float32)
    for group in range(groups):
        picked += jnp.where(place == group, found[group * rows : (group + 1) * rows], 0.0)
    found_ref[...] = picked


def finish_of(bus, plant_bus, terms):
    rows, width = terms[0].shape
    short = -rows % 8
    if short:
        terms = [jnp.pad(term, ((0, short), (0, 0))) for term in terms]
    plants = plant_bus.shape[0]
    whole = pl.BlockSpec((rows + short, width), lambda i: (0, 0))
    grad, found = pl.pallas_call(
        finish_kernel,
        grid=(1,),
        in_specs=[pl.BlockSpec(memory_space=pltpu.SMEM), pl.BlockSpec((1, plants), lambda i: (0, 0))]
        + [whole] * len(terms),
        out_specs=[whole, pl.BlockSpec((rows + short, plants), lambda i: (0, 0))],
        out_shape=[
            jax.ShapeDtypeStruct((rows + short, width), jnp.float32),
            jax.ShapeDtypeStruct((rows + short, plants), jnp.float32),
        ],
        compiler_params=vmem(48),
        cost_estimate=FREE,
        name="finish",
    )(bus, plant_bus[None, :], *terms)
    return (grad[:rows], found[:rows]) if short else (grad, found)


def total_of(terms):
    return sum(term.astype(jnp.float32) for term in terms).astype(jnp.bfloat16)


def make_shards(box, buses):
    steps = plan(box)
    targets = {step_back(step[3], step[1], step[2], box) for step in steps if step[0] == REDUCE}
    own = (0, 0, 0)

    def shards(net_load, release, plant_bus, efficiency, ptdf, branch_class, class_limit, class_price):
        rows = net_load.shape[0]
        bus = lax.axis_index("bus").astype(jnp.int32)[None]
        inject = inject_of(bus, net_load, release, efficiency, plant_bus)
        onehot = (branch_class[:, None] == jnp.arange(class_limit.shape[0])[None, :]).astype(jnp.float32)
        limit = jnp.sum(onehot * class_limit[None, :], axis=1)[None, :]
        price = jnp.sum(onehot * class_price[None, :], axis=1)[None, :]

        def over_bus(value):
            if buses == 2:
                return value, lax.ppermute(value, "bus", [(0, 1), (1, 0)])
            return lax.psum(value, "bus"), jnp.zeros_like(value)

        have, terms, flows, over = {own: inject}, {}, {}, []
        for step in steps:
            if step[0] == FLOWS:
                _, batch, labels, waits = step
                blocks = [have[label] for label in labels]
                blocks[-1] = after(blocks[-1], [over[i] for i in waits])
                flows[batch] = labels, over_bus(flows_of(blocks, ptdf))
                over.append(flows[batch][1][0])
            elif step[0] == GRADS:
                labels, sides = flows[step[1]]
                types = [jnp.float32 if label in targets else jnp.bfloat16 for label in labels]
                parts = grads_of(*sides, limit, price, ptdf, rows, types)
                terms.update((label, [part]) for label, part in zip(labels, parts))
                over.append(parts[0])
            else:
                kind, axis, shift, label, waits = step
                near = step_back(label, axis, shift, box)
                block = have[near] if kind == GATHER else total_of(terms[label])
                waits = [over[i] for i in waits]
                pairs = moves(axis, shift if kind == GATHER else -shift, box)
                with jax.named_scope(f"send_{len(over)}"):
                    came = lax.ppermute(after(block, waits), "br", pairs)
                if kind == GATHER:
                    have[label] = came
                else:
                    terms[near].append(came)
                over.append(came)
        grad_bus, found = finish_of(bus, plant_bus, terms[own])
        mine, other = over_bus(found)
        grad_release = (mine + other) * efficiency[None, :]
        return (grad_bus, grad_release)

    return shards


def solution(mesh):
    placed = (P("br", "bus"), P("br", None), P(), P(), P("br", "bus"), P("br"), P(), P())
    return jax.shard_map(
        make_shards(chip_box(mesh.shape["br"]), mesh.shape["bus"]),
        mesh=mesh,
        in_specs=placed,
        out_specs=(P("br", "bus"), P("br", None)),
        check_vma=False,
    )
```

```python
import functools

import jax
import jax.numpy as jnp
from jax import lax
from jax.experimental import pallas as pl
from jax.experimental.pallas import tpu as pltpu
from jax.sharding import PartitionSpec as P

SMOOTH = 0.25
Z, Y, X = 0, 1, 2
GATHER, REDUCE, FLOWS, GRADS = 0, 1, 2, 3


def chip_box(count):
    bits = (count // 2).bit_length() - 1
    nx = 1 << (bits // 2)
    return count // (2 * nx), 2, nx


PLAN = [
    (GATHER, Z, 1, (1, 0, 0), ()),
    (GATHER, X, 1, (0, 0, 1), ()),
    (GATHER, Y, 1, (0, 1, 0), ()),
    (GATHER, Z, 1, (2, 0, 0), (0,)),
    (GATHER, X, 1, (1, 0, 1), (1,)),
    (GATHER, Y, 1, (0, 1, 1), (2,)),
    (GATHER, Z, -1, (-1, 0, 1), (3,)),
    (GATHER, X, 1, (2, 0, 1), (4,)),
    (GATHER, Y, 1, (1, 1, 1), (5,)),
    (FLOWS, 0, [(0, 0, 0), (1, 0, 0), (0, 0, 1), (0, 1, 0), (2, 0, 0), (1, 0, 1), (0, 1, 1), (-1, 0, 1), (2, 0, 1), (1, 1, 1)], ()),
    (GRADS, 0),
    (GATHER, Z, -1, (-1, 1, 1), (6,)),
    (GATHER, X, 1, (-1, 0, 0), (7,)),
    (GATHER, Y, 1, (2, 1, 1), (8,)),
    (GATHER, Z, -1, (-1, 1, 0), (9, 11)),
    (GATHER, X, 1, (1, 1, 0), (9, 12)),
    (GATHER, Y, 1, (2, 1, 0), (9, 13)),
    (FLOWS, 1, [(-1, 1, 1), (-1, 0, 0), (2, 1, 1), (-1, 1, 0), (1, 1, 0), (2, 1, 0)], ()),
    (GRADS, 1),
    (REDUCE, Y, 1, (0, 1, 1), (16,)),
    (REDUCE, X, 1, (1, 1, 1), (15,)),
    (REDUCE, Z, 1, (1, 0, 0), (14,)),
    (REDUCE, Y, 1, (2, 1, 1), (17, 19)),
    (REDUCE, X, 1, (-1, 1, 1), (17, 20)),
    (REDUCE, Z, 1, (1, 0, 1), (17, 21)),
    (REDUCE, Y, 1, (2, 1, 0), (22,)),
    (REDUCE, X, 1, (2, 0, 1), (23,)),
    (REDUCE, Z, 1, (1, 1, 0), (24,)),
    (REDUCE, Y, 1, (-1, 1, 0), (25,)),
    (REDUCE, X, 1, (-1, 0, 1), (26,)),
    (REDUCE, Z, -1, (2, 0, 0), (27,)),
    (REDUCE, Y, 1, (0, 1, 0), (28,)),
    (REDUCE, X, 1, (0, 0, 1), (29,)),
    (REDUCE, Z, -1, (-1, 0, 0), (30,)),
]


def greedy(box):
    labels = [(z, y, x) for z in range(box[0]) for y in range(box[1]) for x in range(box[2])]
    have, sends = {(0, 0, 0)}, []
    while len(have) < len(labels):
        taken = set()
        for axis in (Z, X, Y):
            shifts = (1, -1) if box[axis] > 2 else (1,)
            options = [
                (shift, label)
                for label in labels
                if label not in have and label not in taken
                for shift in shifts
                if step_back(label, axis, shift, box) in have
            ]
            if options:
                shift, label = options[0]
                sends.append((axis, shift, label))
                taken.add(label)
        have |= taken
    return sends


def step_back(label, axis, shift, box):
    moved = list(label)
    moved[axis] = (moved[axis] - shift) % box[axis]
    return tuple(moved)


def plan(box):
    if box == (4, 2, 2):
        wrap = lambda label: tuple(c % n for c, n in zip(label, box))
        steps = []
        for step in PLAN:
            if step[0] in (GATHER, REDUCE):
                step = (*step[:3], wrap(step[3]), step[4])
            elif step[0] == FLOWS:
                step = (*step[:2], [wrap(label) for label in step[2]], step[3])
            steps.append(step)
        return steps
    sends = greedy(box)
    steps = [(GATHER, *send, ()) for send in sends]
    steps += [(FLOWS, 0, [(0, 0, 0)] + [label for _, _, label in sends], ()), (GRADS, 0)]
    return steps + [(REDUCE, *send, ()) for send in reversed(sends)]


def moves(axis, shift, box):
    pairs = []
    for z in range(box[0]):
        for y in range(box[1]):
            for x in range(box[2]):
                to = step_back((z, y, x), axis, -shift, box)
                pairs.append(((z * box[1] + y) * box[2] + x, (to[0] * box[1] + to[1]) * box[2] + to[2]))
    return pairs


def after(value, earlier):
    if not earlier:
        return value
    return lax.optimization_barrier((value, *earlier))[0]


def tile_of(width, group):
    groups = width // group
    return group * max(n for n in range(1, 65) if groups % n == 0)


GROUP = 256


def scatter_lanes(column):
    lane = lax.broadcasted_iota(jnp.int32, (GROUP, column.shape[1]), 0)
    return jnp.where(lane == column % GROUP, 1.0, 0.0).astype(jnp.bfloat16)


def split_high(value):
    high = value.astype(jnp.bfloat16)
    return high, (value - high.astype(jnp.float32)).astype(jnp.bfloat16)


def place_of(bus_ref, column, groups):
    tile = bus_ref[0] * pl.num_programs(0) + pl.program_id(0)
    return column // GROUP - tile * groups


def inject_kernel(bus_ref, release_ref, efficiency_ref, plant_ref, net_ref, out_ref):
    rows, width = net_ref.shape
    groups = width // GROUP
    column = plant_ref[...]
    lanes = scatter_lanes(column)
    place = place_of(bus_ref, column, groups)

    def spread(values):
        picked = [jnp.where(place == group, values, 0.0) for group in range(groups)]
        return lax.dot_general(
            jnp.concatenate(picked, axis=0).astype(jnp.bfloat16),
            lanes,
            (((1,), (1,)), ((), ())),
            preferred_element_type=jnp.float32,
        )

    high, low = split_high(release_ref[...] * efficiency_ref[...])
    added = spread(high.astype(jnp.float32)) + spread(low.astype(jnp.float32))
    for group in range(groups):
        at = slice(group * GROUP, (group + 1) * GROUP)
        total = net_ref[:, at].astype(jnp.float32) + added[group * rows : (group + 1) * rows]
        out_ref[:, at] = total.astype(jnp.bfloat16)


FREE = pl.CostEstimate(flops=0, bytes_accessed=0, transcendentals=0)


def vmem(mebibytes):
    return pltpu.CompilerParams(vmem_limit_bytes=mebibytes << 20)


def inject_of(bus, net_load, release, efficiency, plant_bus):
    rows, width = net_load.shape
    short = -rows % 8
    if short:
        net_load = jnp.pad(net_load, ((0, short), (0, 0)))
        release = jnp.pad(release, ((0, short), (0, 0)))
    tile = tile_of(width, GROUP)
    plants = release.shape[1]
    whole = pl.BlockSpec((1, plants), lambda i: (0, 0))
    tiled = pl.BlockSpec((rows + short, tile), lambda i: (0, i))
    out = pl.pallas_call(
        inject_kernel,
        grid=(width // tile,),
        in_specs=[
            pl.BlockSpec(memory_space=pltpu.SMEM),
            pl.BlockSpec((rows + short, plants), lambda i: (0, 0)),
            whole,
            whole,
            tiled,
        ],
        out_specs=tiled,
        out_shape=jax.ShapeDtypeStruct(net_load.shape, jnp.bfloat16),
        compiler_params=vmem(60),
        cost_estimate=FREE,
        name="inject",
    )(bus, release, efficiency[None, :], plant_bus[None, :], net_load)
    return out[:rows] if short else out


RESIDENT = pl.BlockSpec(memory_space=pltpu.VMEM)


def flows_kernel(tile, *refs):
    *blocks, ptdf_ref, out_ref = refs
    total = jnp.zeros(out_ref.shape[::-1], jnp.float32)

    def add(i, total):
        at = pl.ds(pl.multiple_of(i * tile, 128), tile)
        rows = jnp.concatenate([block[:, at].astype(jnp.float32) for block in blocks], axis=0)
        return total + lax.dot_general(
            ptdf_ref[:, at], rows.astype(jnp.bfloat16), (((1,), (1,)), ((), ())), preferred_element_type=jnp.float32
        )

    out_ref[...] = lax.fori_loop(0, ptdf_ref.shape[1] // tile, add, total).T


def flows_of(blocks, ptdf):
    rows = blocks[0].shape[0]
    branches, width = ptdf.shape
    if rows % 8:
        short = -rows * len(blocks) % 8
        blocks = [jnp.pad(jnp.concatenate(blocks, axis=0), ((0, short), (0, 0)))]
        rows = blocks[0].shape[0]
    count = len(blocks)
    return pl.pallas_call(
        functools.partial(flows_kernel, tile_of(width, 128)),
        in_specs=[RESIDENT] * (count + 1),
        out_specs=RESIDENT,
        out_shape=jax.ShapeDtypeStruct((count * rows, branches), jnp.float32),
        compiler_params=vmem(16),
        cost_estimate=FREE,
        name="flows",
    )(*blocks, ptdf)


def grad_flow_of(flows, limit, price):
    upper = jax.nn.sigmoid((flows - limit) / SMOOTH)
    lower = jax.nn.sigmoid((-flows - limit) / SMOOTH)
    return (price * (upper - lower)).astype(jnp.bfloat16)


def grads_kernel(tile, mine_ref, other_ref, limit_ref, price_ref, ptdf_ref, *out_refs):
    rows = out_refs[0].shape[0]
    grad_flow = grad_flow_of(mine_ref[...] + other_ref[...], limit_ref[...], price_ref[...])

    @pl.loop(0, ptdf_ref.shape[1] // tile)
    def _(i):
        at = pl.ds(pl.multiple_of(i * tile, 128), tile)
        grads = jnp.dot(grad_flow, ptdf_ref[:, at], preferred_element_type=jnp.float32)
        for index, out_ref in enumerate(out_refs):
            out_ref[:, at] = grads[index * rows : (index + 1) * rows].astype(out_ref.dtype)


def grads_of(mine, other, limit, price, ptdf, rows, types):
    width = ptdf.shape[1]
    if rows % 8:
        grads = jnp.dot(grad_flow_of(mine + other, limit, price), ptdf, preferred_element_type=jnp.float32)
        return [grads[i * rows : (i + 1) * rows] for i in range(len(types))]
    return pl.pallas_call(
        functools.partial(grads_kernel, tile_of(width, 128)),
        in_specs=[RESIDENT] * 5,
        out_specs=[RESIDENT] * len(types),
        out_shape=[jax.ShapeDtypeStruct((rows, width), dtype) for dtype in types],
        compiler_params=vmem(16),
        cost_estimate=FREE,
        name="grads",
    )(mine, other, limit, price, ptdf)


def finish_kernel(bus_ref, plant_ref, *refs):
    *terms, grad_ref, found_ref = refs
    rows, width = grad_ref.shape
    groups = width // GROUP
    column = plant_ref[...]
    lanes = scatter_lanes(column)
    grad = sum(term[...].astype(jnp.float32) for term in terms)
    grad_ref[...] = grad
    place = place_of(bus_ref, column, groups)
    high, low = split_high(jnp.concatenate([grad[:, g * GROUP : (g + 1) * GROUP] for g in range(groups)], axis=0))
    found = jnp.dot(
        jnp.concatenate([high, low], axis=1),
        jnp.concatenate([lanes, lanes], axis=0),
        preferred_element_type=jnp.float32,
    )
    picked = jnp.zeros(found_ref.shape, jnp.float32)
    for group in range(groups):
        picked += jnp.where(place == group, found[group * rows : (group + 1) * rows], 0.0)
    found_ref[...] = picked


def finish_of(bus, plant_bus, terms):
    rows, width = terms[0].shape
    short = -rows % 8
    if short:
        terms = [jnp.pad(term, ((0, short), (0, 0))) for term in terms]
    plants = plant_bus.shape[0]
    whole = pl.BlockSpec((rows + short, width), lambda i: (0, 0))
    grad, found = pl.pallas_call(
        finish_kernel,
        grid=(1,),
        in_specs=[pl.BlockSpec(memory_space=pltpu.SMEM), pl.BlockSpec((1, plants), lambda i: (0, 0))]
        + [whole] * len(terms),
        out_specs=[whole, pl.BlockSpec((rows + short, plants), lambda i: (0, 0))],
        out_shape=[
            jax.ShapeDtypeStruct((rows + short, width), jnp.float32),
            jax.ShapeDtypeStruct((rows + short, plants), jnp.float32),
        ],
        compiler_params=vmem(48),
        cost_estimate=FREE,
        name="finish",
    )(bus, plant_bus[None, :], *terms)
    return (grad[:rows], found[:rows]) if short else (grad, found)


def total_of(terms):
    return sum(term.astype(jnp.float32) for term in terms).astype(jnp.bfloat16)


def make_shards(box, buses):
    steps = plan(box)
    targets = {step_back(step[3], step[1], step[2], box) for step in steps if step[0] == REDUCE}
    own = (0, 0, 0)

    def shards(net_load, release, plant_bus, efficiency, ptdf, branch_class, class_limit, class_price):
        rows = net_load.shape[0]
        bus = lax.axis_index("bus").astype(jnp.int32)[None]
        inject = inject_of(bus, net_load, release, efficiency, plant_bus)
        onehot = (branch_class[:, None] == jnp.arange(class_limit.shape[0])[None, :]).astype(jnp.float32)
        limit = jnp.sum(onehot * class_limit[None, :], axis=1)[None, :]
        price = jnp.sum(onehot * class_price[None, :], axis=1)[None, :]

        def over_bus(value):
            if buses == 2:
                return value, lax.ppermute(value, "bus", [(0, 1), (1, 0)])
            return lax.psum(value, "bus"), jnp.zeros_like(value)

        have, terms, flows, over = {own: inject}, {}, {}, []
        for step in steps:
            if step[0] == FLOWS:
                _, batch, labels, waits = step
                blocks = [have[label] for label in labels]
                blocks[-1] = after(blocks[-1], [over[i] for i in waits])
                flows[batch] = labels, over_bus(flows_of(blocks, ptdf))
                over.append(flows[batch][1][0])
            elif step[0] == GRADS:
                labels, sides = flows[step[1]]
                types = [jnp.float32 if label in targets else jnp.bfloat16 for label in labels]
                parts = grads_of(*sides, limit, price, ptdf, rows, types)
                terms.update((label, [part]) for label, part in zip(labels, parts))
                over.append(parts[0])
            else:
                kind, axis, shift, label, waits = step
                near = step_back(label, axis, shift, box)
                block = have[near] if kind == GATHER else total_of(terms[label])
                waits = [over[i] for i in waits]
                pairs = moves(axis, shift if kind == GATHER else -shift, box)
                with jax.named_scope(f"send_{len(over)}"):
                    came = lax.ppermute(after(block, waits), "br", pairs)
                if kind == GATHER:
                    have[label] = came
                else:
                    terms[near].append(came)
                over.append(came)
        grad_bus, found = finish_of(bus, plant_bus, terms[own])
        mine, other = over_bus(found)
        grad_release = (mine + other) * efficiency[None, :]
        return (grad_bus, grad_release)

    return shards


def solution(mesh):
    placed = (P("br", "bus"), P("br", None), P(), P(), P("br", "bus"), P("br"), P(), P())
    return jax.shard_map(
        make_shards(chip_box(mesh.shape["br"]), mesh.shape["bus"]),
        mesh=mesh,
        in_specs=placed,
        out_specs=(P("br", "bus"), P("br", None)),
        check_vma=False,
    )
```
